32 devices in a mesh: expert: 4 (over z), mp: 4 (over y, core), replica: 2 (over x).
Axes of the slice: x: 2, y: 2, z: 4, core: 2. Of those that a mesh axis runs over, the one named last changes fastest.
Arguments:
- grad_out: bfloat16 [2, 512, 2080], P('replica', 'expert')
- route: int32 [2, 512, 1], P('replica', 'expert'), may hold values from 0 to 3; in each aligned block of 128 rows (0 to 127, 128 to 255, ..., all dimensions but the last counted through in order) at most 48 rows name the same one
- hidden_act: bfloat16 [2, 4, 192, 6144], P('replica', 'expert', None, 'mp'), as said below
- out_weight: bfloat16 [4, 6144, 2080], P('expert', 'mp'), may hold values from -0.078125 to 0.078125
- row_state: float32 [4, 6144], P('expert', ('mp', 'replica')), may hold values from 0.01 to 0.3
- col_state: float32 [4, 2080], P('expert'), as said below
Outputs:
- hidden_grad: bfloat16 [2, 4, 192, 6144], P('replica', 'expert', None, 'mp')
- update: float32 [4, 6144, 2080], P('expert', ('mp', 'replica'))
- row_new: float32 [4, 6144], P('expert', ('mp', 'replica'))
- col_new: float32 [4, 2080], P('expert')
The draws below stay inside these ranges and needn't reach their ends.
Inputs may be any that keep to these rules, and one draw needn't show every extreme that they name: `route`: in each aligned block of 128 tokens (the tokens of one index of expert) no expert is named more than 48 times, a bound that some block reaches. `hidden_act`: non-negative. `col_state`: positive.
All inputs are finite; a program needn't handle non-finite values.
Results may differ from the reference program's by a relative error of at most 0.001.
Values may be sent and summed in bfloat16 or wider, within the bound.
A program may use at most 128 MiB of HBM per device.

```python
import math
import jax
import jax.numpy as jnp
import numpy as np
from jax import lax

D = 2080
FF = 6144
EXP_DEV = 1
TOK_DEV = 128
EXPERTS = 4
CAP = 48
SLOTS = 192
GROUP_TOK = 512
N_EXPERT = 4
N_REPLICA = 2


def draw_hidden_act(key, part):
    key = jax.random.fold_in(key, 11)
    key_values, key_scale = jax.random.split(key)
    trend = 3.0 ** (jnp.arange(FF, dtype=jnp.float32) / FF)
    col_scale = jnp.exp(jax.random.uniform(key_scale, (FF,), jnp.float32) * math.log(10.0)) * trend
    base_values = jax.random.uniform(key_values, (N_REPLICA, EXPERTS, SLOTS, FF), jnp.float32)
    return (base_values * col_scale / 100.0).astype(jnp.bfloat16)


def draw_grad_out(key, part):
    key = jax.random.fold_in(key, 12)
    key_values, key_scale = jax.random.split(key)
    col_scale = jnp.exp(jax.random.uniform(key_scale, (D,), jnp.float32) * math.log(10.0)) / 4.6
    base_values = jax.random.normal(key_values, (N_REPLICA, GROUP_TOK, D), jnp.float32)
    return (base_values * col_scale).astype(jnp.bfloat16)


def draw_col_state(key, part):
    key = jax.random.fold_in(key, 13)
    key_order, key_values = jax.random.split(key)
    order = jax.random.permutation(key_order, EXPERTS).astype(jnp.float32)
    spread = 10.0 ** ((2.0 * order + 1.0) / EXPERTS - 1.0)
    level = 0.00265 * TOK_DEV * N_REPLICA / EXP_DEV
    values = jnp.exp(jax.random.uniform(key_values, (EXPERTS, D), jnp.float32, math.log(0.5), math.log(2.0)))
    return (values * spread[:, None] * level).astype(jnp.float32)


def level_of(key, shape, shards, least, largest):
    gain, own = 1.0, jax.random.fold_in(key, 6)
    for dim, shards_of in shards:
        steps = jnp.exp(jax.random.uniform(jax.random.fold_in(own, dim), (shards_of,), jnp.float32, least / len(shards), largest / len(shards)))
        gain = gain * jnp.repeat(steps, shape[dim] // shards_of).reshape([-1 if axis == dim else 1 for axis in range(len(shape))])
    return gain


def shared_out(rng, own, number, rows, amount, top, reach, lean):
    ranking = jax.random.permutation(rng, amount)
    crowded, usual = shares(amount, rows * top, reach, lean, True), shares(amount, rows * top, reach, lean, False)
    places = jnp.arange(amount)

    def named(lengths, offset_by):
        used = int((lengths > 0).sum())
        fixed = max(1, used // 4)
        shifted = fixed + (places - fixed + offset_by * (used - fixed)) % max(1, amount - fixed)
        return jnp.zeros((amount,), jnp.int32).at[ranking[jnp.where(places < fixed, places, shifted)]].set(jnp.asarray(lengths, jnp.int32))

    lengths = jnp.where(number % 4 == 0, named(crowded, number // 4), named(usual, number - number // 4 - 1))
    mixed = jax.random.permutation(jax.random.fold_in(own, 3), amount)
    source_of, taker = mixed[0:amount // 2 * 2:2], mixed[1:amount // 2 * 2:2]
    margin = jnp.minimum(lengths[source_of] - 1, reach - lengths[taker]) // 2
    margin = jnp.where((source_of == ranking[0]) | (taker == ranking[0]) | (lengths[taker] == 0), 0, jnp.maximum(margin, 0))
    shifted = jax.random.randint(jax.random.fold_in(own, 4), (amount // 2,), 0, 1 << 20) % (margin + 1)
    lengths = lengths.at[source_of].add(-shifted).at[taker].add(shifted)
    items = jnp.searchsorted(jnp.cumsum(lengths), jnp.arange(rows * top), side="right").astype(jnp.int32)
    grid = items.reshape(top, rows).T
    grid = grid[jax.random.permutation(jax.random.fold_in(own, 1), rows)]
    offset_by = jax.random.randint(jax.random.fold_in(own, 2), (rows, 1), 0, top)
    return jnp.take_along_axis(grid, (jnp.arange(top)[None, :] + offset_by) % top, axis=1)


def shares(count, total, bound, lean, full):
    portions = [(1 << 20) // math.isqrt(rank ** lean) + 1 for rank in range(1, count + 1)]
    largest = bound if full else min(bound, max(-(-total // count), total * portions[0] // sum(portions)))
    least = 1 if total - largest >= count - 1 else 0
    counts, spare = [largest] + [least] * (count - 1), total - largest - least * (count - 1)
    while spare > 0:
        candidates = [i for i in range(1, count) if counts[i] < largest] or [i for i in range(1, count) if counts[i] < bound]
        whole, budget = sum([portions[i] for i in candidates]), spare
        for i in candidates:
            extra = min(bound - counts[i], max(1, budget * portions[i] // whole), spare)
            counts[i] = counts[i] + extra
            spare = spare - extra
    return np.array(counts)


def bell_draw(rng, extent, scale, bound, pieces=(), held_as=jnp.bfloat16):
    result = jax.random.normal(rng, extent, jnp.float32) * scale
    if len(pieces) > 0:
        result = level_of(rng, extent, pieces, -0.22, 0.18) * result
    return jnp.clip(result, min=-bound, max=bound).astype(held_as)


def setup_inputs(seed: int = 0) -> dict:
    arg_keys = jax.random.split(jax.random.key(seed), 7)
    grad_out = draw_grad_out(jax.random.fold_in(arg_keys[6], 71), 0)
    route_keys = jax.random.split(jax.random.fold_in(arg_keys[1], 1), N_REPLICA * GROUP_TOK // TOK_DEV)
    route_turns = jax.random.permutation(jax.random.fold_in(arg_keys[1], 3), N_REPLICA * GROUP_TOK // TOK_DEV)
    route = jax.vmap(lambda own, number: shared_out(jax.random.fold_in(arg_keys[1], 2), own, number, TOK_DEV, EXPERTS, 1, CAP, 2))(route_keys, route_turns).reshape((N_REPLICA, GROUP_TOK, 1))
    hidden_act = draw_hidden_act(jax.random.fold_in(arg_keys[6], 71), 0)
    out_weight = bell_draw(arg_keys[3], (EXPERTS, FF, D), FF ** -0.5, 0.078125, ((0, 4), (1, 4)))
    row_state = jnp.clip(jnp.exp(math.log(0.3) - 3.4011974 * jax.random.uniform(arg_keys[4], (EXPERTS, FF), jnp.float32) ** level_of(arg_keys[4], (EXPERTS, FF), ((0, 4), (1, 8)), -0.2, 0.2)), 0.01, 0.3)
    col_state = draw_col_state(jax.random.fold_in(arg_keys[6], 71), 0)
    return dict(grad_out=grad_out, route=route, hidden_act=hidden_act, out_weight=out_weight, row_state=row_state, col_state=col_state)


decay_rate = 0.8
clip_limit = 1.0
tiny_square = 1e-30

def place_tokens(tokens, expert_ids, experts):
    blocks = expert_ids.reshape(N_EXPERT, TOK_DEV)
    onehot = (blocks[:, :, None] == jnp.arange(experts, dtype=jnp.int32)[None, None, :]).astype(jnp.int32)
    position = lax.optimization_barrier(jnp.sum((jnp.cumsum(onehot, axis=1) - onehot) * onehot, axis=2))
    slot_index = (jnp.arange(N_EXPERT, dtype=jnp.int32)[:, None] * CAP + position).reshape(-1).astype(jnp.int32)
    empty = jnp.zeros((experts, SLOTS, D), jnp.bfloat16)
    return empty.at[expert_ids, slot_index].set(tokens)

def one_expert(inputs):
    arrived, hidden, weight, row_old, col_old = inputs
    flat_arrived = arrived.reshape(-1, D)
    flat_hidden = hidden.reshape(-1, FF)
    hidden_grad = jnp.dot(flat_arrived, weight.T, preferred_element_type=jnp.float32).astype(jnp.bfloat16)
    grad = jnp.dot(flat_hidden.T, flat_arrived, preferred_element_type=jnp.float32)
    squares = grad * grad + tiny_square
    row_new = decay_rate * row_old + (1.0 - decay_rate) * lax.optimization_barrier(jnp.mean(squares, axis=1))
    col_new = decay_rate * col_old + (1.0 - decay_rate) * lax.optimization_barrier(jnp.mean(squares, axis=0))
    raw_step = grad / jnp.sqrt(row_new[:, None] * col_new[None, :] / jnp.mean(row_new))
    update_rms = jnp.sqrt(jnp.mean(raw_step * raw_step))
    update = raw_step / jnp.maximum(1.0, update_rms / clip_limit)
    return (hidden_grad.reshape(N_REPLICA, SLOTS, FF), update, row_new, col_new)

def reference(grad_out, route, hidden_act, out_weight, row_state, col_state):
    experts = out_weight.shape[0]
    received = jnp.stack([place_tokens(grad_out[member], route[member, :, 0], experts) for member in range(N_REPLICA)])
    hidden_grad, update, row_new, col_new = lax.map(one_expert, (received.transpose(1, 0, 2, 3), hidden_act.transpose(1, 0, 2, 3), out_weight, row_state, col_state))
    return (hidden_grad.transpose(1, 0, 2, 3), update, row_new, col_new)
```

```python
import functools

import jax
import jax.numpy as jnp
from jax import lax
from jax.experimental import pallas as pl
from jax.experimental.pallas import tpu as pltpu
from jax.sharding import PartitionSpec as P

FF = 6144
EXP_DEV = 1


decay_rate = 0.8
clip_limit = 1.0
tiny_square = 1e-30


def on_device(grad_out, route, hidden_act, out_weight, row_state, col_state):
    n_expert = lax.axis_size("expert")
    tok_count = grad_out.shape[1]
    width = grad_out.shape[2]
    experts = EXP_DEV * n_expert
    capacity = 3 * tok_count // (2 * experts)
    tokens = grad_out[0]
    expert_ids = route[0, :, 0]
    onehot = (expert_ids[:, None] == jnp.arange(experts, dtype=jnp.int32)[None, :]).astype(
        jnp.float32
    )
    row_iota = lax.broadcasted_iota(jnp.int32, (tok_count, tok_count), 0)
    col_iota = lax.broadcasted_iota(jnp.int32, (tok_count, tok_count), 1)
    earlier = (row_iota > col_iota).astype(jnp.float32)
    position = jnp.sum(
        jnp.dot(earlier, onehot, preferred_element_type=jnp.float32) * onehot, axis=1
    ).astype(jnp.int32)
    slot_index = expert_ids * capacity + position
    dispatch = (
        slot_index[None, :] == jnp.arange(experts * capacity, dtype=jnp.int32)[:, None]
    ).astype(jnp.bfloat16)
    outgoing = jnp.dot(dispatch, tokens, preferred_element_type=jnp.float32).astype(jnp.bfloat16)
    outgoing = outgoing.reshape(n_expert, EXP_DEV * capacity, width)
    arrived = lax.all_to_all(outgoing, "expert", split_axis=0, concat_axis=0, tiled=True)
    arrived = arrived.reshape(n_expert, EXP_DEV, capacity, width).transpose(1, 0, 2, 3)
    arrived = arrived.reshape(EXP_DEV, n_expert * capacity, width)
    hidden = hidden_act[0]
    hidden_grad = jnp.einsum(
        "esd,efd->esf", arrived, out_weight, preferred_element_type=jnp.float32
    )
    hidden_grad = hidden_grad.astype(jnp.bfloat16)[None]
    parts = lax.all_to_all(hidden, "replica", split_axis=2, concat_axis=1, tiled=True)
    grad = jnp.einsum(
        "esf,esd->efd",
        parts,
        lax.all_gather(arrived, "replica", axis=1, tiled=True),
        preferred_element_type=jnp.float32,
    )
    squares = grad * grad + tiny_square
    row_new = decay_rate * row_state + (1.0 - decay_rate) * jnp.mean(squares, axis=2)
    col_part = jnp.sum(squares, axis=1)
    row_part = jnp.sum(row_new, axis=1)
    weighted = jnp.sum(grad * grad / row_new[:, :, None], axis=1)
    col_total, weighted_total, row_total = lax.psum(
        (col_part, weighted, row_part), ("mp", "replica")
    )
    col_new = decay_rate * col_state + (1.0 - decay_rate) * col_total / FF
    row_mean = row_total / FF
    raw_step = grad / jnp.sqrt(row_new[:, :, None] * col_new[:, None, :] / row_mean[:, None, None])
    update_sq = row_mean * jnp.sum(weighted_total / col_new, axis=1)
    update_rms = jnp.sqrt(update_sq / (FF * width))
    update = raw_step / jnp.maximum(1.0, update_rms / clip_limit)[:, None, None]
    return (hidden_grad, update, row_new, col_new)


MESH = pl.DeviceIdType.MESH
CH = 512
REM = 128


def exchange_kernel(
    n, cap, tok_ref, ids_ref, hid_ref, w_hbm, row_ref, col_ref,
    hg_ref, rownew_ref, colnew_ref, cfac_ref, rfac_ref, ht_hbm, rec_hbm,
    outb, zb, parts, hs, ht, w, st, rowcol, w_sem, loc_sem, send_sem, recv_sem,
):
    e = lax.axis_index("expert")
    m = lax.axis_index("mp")
    r = lax.axis_index("replica")
    width = tok_ref.shape[1]
    slots = n * cap
    half = hs.shape[1]
    rem = width - 4 * CH
    f32 = jnp.float32

    w_copy = pltpu.make_async_copy(w_hbm, w, w_sem)
    w_copy.start()

    def across(d):
        m2 = m + (1 - 2 * (m % 2)) * (d % 2)
        m2 = m2 + (2 - 4 * (m // 2)) * ((d // 2) % 2)
        r2 = r + (1 - 2 * r) * (d // 4)
        return (e, m2, r2)

    def along(k):
        return (lax.rem(e + k, n), m, r)

    barrier = pltpu.get_barrier_semaphore()
    for d in range(1, 8):
        pl.semaphore_signal(barrier, inc=1, device_id=across(d), device_id_type=MESH)
    for k in range(1, n):
        pl.semaphore_signal(barrier, inc=1, device_id=along(k), device_id_type=MESH)

    tc = tok_ref.shape[0]
    ids = jnp.broadcast_to(ids_ref[...].astype(f32), (tc, tc))
    ids_t = ids.T
    p_i = lax.broadcasted_iota(jnp.int32, (tc, tc), 0)
    q_i = lax.broadcasted_iota(jnp.int32, (tc, tc), 1)
    before = jnp.where((p_i < q_i) & (ids == ids_t), 1.0, 0.0)
    slot = ids_t[0:1, :] * cap + jnp.sum(before, axis=0, keepdims=True)
    want = lax.broadcasted_iota(jnp.int32, (slots, tc), 0).astype(f32)
    dispatch = jnp.where(want == slot, 1.0, 0.0).astype(jnp.bfloat16)
    mine = tok_ref[:, pl.ds(pl.multiple_of(m * CH, CH), CH)]
    outb[:, 0:CH] = jnp.dot(dispatch, mine, preferred_element_type=f32).astype(jnp.bfloat16)
    outb[:, CH:] = jnp.zeros((slots, REM), jnp.bfloat16)
    outb[:, CH:CH + rem] = jnp.dot(
        dispatch, tok_ref[:, 4 * CH:], preferred_element_type=f32
    ).astype(jnp.bfloat16)
    pl.semaphore_wait(barrier, 7 + n - 1)

    started = []

    def send(src, dst, to):
        i = len(started)
        c = pltpu.make_async_remote_copy(
            src_ref=src, dst_ref=dst, send_sem=send_sem.at[i], recv_sem=recv_sem.at[i],
            device_id=to, device_id_type=MESH,
        )
        c.start()
        started.append(c)
        return c

    def rows_of(k, base=0):
        return pl.ds(pl.multiple_of(base + lax.rem(e - k + n, n) * cap, 16), cap)

    own = rows_of(0)
    zc = [None]
    for k in range(1, n):
        there = pl.ds(pl.multiple_of(lax.rem(e + k, n) * cap, 16), cap)
        zc.append(send(outb.at[there, :], zb.at[own, :], along(k)))
    zb[own, :] = outb[own, :]
    other_half = pl.ds(pl.multiple_of((1 - r) * half, 128), half)
    own_half = pl.ds(pl.multiple_of(r * half, 128), half)
    xc, hc, yo, co = [], [], [], []
    for k in range(n):
        if k:
            zc[k].wait_recv()
        a, b = rows_of(k), rows_of(k, slots)
        xc.append(send(zb.at[a, :], zb.at[b, :], across(4)))
        yo.append(send(zb.at[a, 0:CH], parts.at[m, a, :], across(2)))
        co.append(send(zb.at[a, 0:CH], parts.at[m, a, :], across(1)))
        piece = pl.ds(k * cap, cap)
        there = pl.ds(slots + k * cap, cap)
        hc.append(send(hid_ref.at[piece, other_half], hs.at[there, :], across(4)))
    m_y = across(2)[1]
    parts[m, 0:slots, :] = zb[0:slots, 0:CH]
    hs[0:slots, :] = hid_ref[:, own_half]
    fo, yx, cx, fx = [], [], [], []
    for k in range(n):
        yo[k].wait_recv()
        a = rows_of(k)
        fo.append(send(parts.at[m_y, a, :], parts.at[m_y, a, :], across(1)))
    for k in range(n):
        xc[k].wait_recv()
        b = rows_of(k, slots)
        yx.append(send(zb.at[b, 0:CH], parts.at[m, b, :], across(2)))
        cx.append(send(zb.at[b, 0:CH], parts.at[m, b, :], across(1)))
    for k in range(n):
        co[k].wait_recv()
        fo[k].wait_recv()
    w_copy.wait()

    nt = (((1,), (1,)), ((), ()))

    def hidden_tile(t):
        f = pl.ds(pl.multiple_of(t * 256, 256), 256)
        acc = lax.dot_general(
            zb[0:slots, CH:CH + rem], w[f, 4 * CH:], nt, preferred_element_type=f32
        )
        for c in range(4):
            acc += lax.dot_general(
                parts[c, 0:slots, :], w[f, c * CH:(c + 1) * CH], nt, preferred_element_type=f32
            )
        hg_ref[:, f] = acc.astype(jnp.bfloat16)

    tiles = hg_ref.shape[1] // 256
    for k in range(n):
        lo, hi = tiles * k // n, tiles * (k + 1) // n

        def some(t, carry):
            hidden_tile(t)
            return carry

        lax.fori_loop(lo, hi, some, 0)
        yx[k].wait_recv()
        b = rows_of(k, slots)
        fx.append(send(parts.at[m_y, b, :], parts.at[m_y, b, :], across(1)))
    parts[m, slots:, :] = zb[slots:, 0:CH]
    for k in range(n):
        hc[k].wait_recv()
        cx[k].wait_recv()
        fx[k].wait_recv()

    local = []
    for c in range(4):
        local.append(pltpu.make_async_copy(
            parts.at[c], rec_hbm.at[:, pl.ds(c * CH, CH)], loc_sem.at[c]))
    local.append(pltpu.make_async_copy(
        zb.at[:, pl.ds(CH, REM)], rec_hbm.at[:, pl.ds(4 * CH, REM)], loc_sem.at[4]))
    for c in local:
        c.start()

    rowcol[...] = jnp.broadcast_to(row_ref[...], (128, half)).T
    blk = 128

    def block(t, carry):
        total, cols, weights = carry
        i = pl.ds(pl.multiple_of(t * blk, blk), blk)
        h = hs[:, i].T
        ht[i, :] = h
        gg = []
        for c in range(5):
            rhs = parts[c] if c < 4 else zb[:, CH:CH + REM]
            g = jnp.dot(h, rhs, preferred_element_type=f32)
            gg.append(g * g)
        rs = sum(jnp.sum(x, axis=1, keepdims=True) for x in gg)
        mean = rs / width + tiny_square
        new = decay_rate * rowcol[i, 0:1] + (1.0 - decay_rate) * mean
        rfac_ref[i, :] = lax.rsqrt(new)
        rowcol[i, :] = jnp.broadcast_to(new, (blk, 128))
        inv = 1.0 / new
        total = total + jnp.sum(new, axis=0, keepdims=True)
        cols = tuple(
            a + jnp.sum(x, axis=0, keepdims=True) for a, x in zip(cols, gg))
        weights = tuple(
            a + jnp.sum(x * inv, axis=0, keepdims=True) for a, x in zip(weights, gg))
        return total, cols, weights

    zero = tuple(jnp.zeros((1, CH if c < 4 else REM), f32) for c in range(5))
    total, cols, weights = lax.fori_loop(
        0, half // blk, block, (jnp.zeros((1, 1), f32), zero, zero))
    me = m * 2 + r
    cols = [x + half * tiny_square for x in cols]
    for j in range(17):
        c, o = j // 4, (j % 4) * 128
        st[me, j:j + 1, :] = cols[c][:, o:o + 128]
        st[me, 17 + j:18 + j, :] = weights[c][:, o:o + 128]
    st[me, 34:35, :] = jnp.broadcast_to(total, (1, 128))
    st[me, 35:40, :] = jnp.zeros((5, 128), f32)
    sc = [send(st.at[me], st.at[me], across(d)) for d in range(1, 8)]
    ht_copy = pltpu.make_async_copy(ht, ht_hbm, loc_sem.at[5])
    ht_copy.start()
    rownew_ref[...] = rowcol[...].T[0:1, :]
    for c in sc:
        c.wait_recv()
    tot = st[0]
    for j in range(1, 8):
        tot = tot + st[j]

    def flat(base):
        x = jnp.concatenate([tot[base + j:base + j + 1, :] for j in range(17)], axis=1)
        return x[:, 0:width]

    col_new = decay_rate * col_ref[...] + (1.0 - decay_rate) * (flat(0) / FF)
    row_mean = tot[34:35, 0:1] / FF
    colnew_ref[...] = col_new
    ratio = jnp.sum(flat(17) / col_new, axis=1, keepdims=True)
    rms = jnp.sqrt(row_mean * ratio / (FF * width))
    scale = jnp.sqrt(row_mean) / jnp.maximum(1.0, rms / clip_limit)
    cfac_ref[...] = lax.rsqrt(col_new) * scale
    for c in started:
        c.wait_send()
    for c in local:
        c.wait()
    ht_copy.wait()


def update_kernel(ht_ref, rec_ref, rfac_ref, cfac_ref, out_ref):
    width = out_ref.shape[1]
    h = ht_ref[...]
    rf = rfac_ref[...]
    for c in range(5):
        lo, hi = c * CH, min(width, (c + 1) * CH)
        g = jnp.dot(h, rec_ref[:, lo:hi], preferred_element_type=jnp.float32)
        out_ref[:, lo:hi] = (g * rf) * cfac_ref[:, lo:hi]


def fused(grad_out, route, hidden_act, out_weight, row_state, col_state):
    n = lax.axis_size("expert")
    tok_count, width = grad_out.shape[1:]
    cap = 3 * tok_count // (2 * n)
    slots = n * cap
    ff = hidden_act.shape[3]
    half = ff // 2
    bf16, f32 = jnp.bfloat16, jnp.float32
    vmem = pl.BlockSpec(memory_space=pltpu.VMEM)
    hbm = pl.BlockSpec(memory_space=pl.ANY)
    wide = 4 * CH + REM
    copies = 9 * n + n - 1 + 7
    hg, row_new, col_new, cfac, rfac, ht, rec = pl.pallas_call(
        functools.partial(exchange_kernel, n, cap),
        out_shape=[
            jax.ShapeDtypeStruct((slots, ff), bf16),
            jax.ShapeDtypeStruct((1, half), f32),
            jax.ShapeDtypeStruct((1, width), f32),
            jax.ShapeDtypeStruct((1, width), f32),
            jax.ShapeDtypeStruct((half, 1), f32),
            jax.ShapeDtypeStruct((half, 2 * slots), bf16),
            jax.ShapeDtypeStruct((2 * slots, wide), bf16),
        ],
        in_specs=[vmem, vmem, vmem, hbm, vmem, vmem],
        out_specs=[vmem] * 5 + [hbm] * 2,
        scratch_shapes=[
            pltpu.VMEM((slots, CH + REM), bf16),
            pltpu.VMEM((2 * slots, CH + REM), bf16),
            pltpu.VMEM((4, 2 * slots, CH), bf16),
            pltpu.VMEM((2 * slots, half), bf16),
            pltpu.VMEM((half, 2 * slots), bf16),
            pltpu.VMEM((ff, width), bf16),
            pltpu.VMEM((8, 40, 128), f32),
            pltpu.VMEM((half, 128), f32),
            pltpu.SemaphoreType.DMA,
            pltpu.SemaphoreType.DMA((6,)),
            pltpu.SemaphoreType.DMA((copies,)),
            pltpu.SemaphoreType.DMA((copies,)),
        ],
        compiler_params=pltpu.CompilerParams(
            collective_id=0, has_side_effects=True, vmem_limit_bytes=40 * 1024 * 1024
        ),
    )(grad_out[0], route[0], hidden_act[0, 0], out_weight[0], row_state, col_state)
    blk = 128
    update = pl.pallas_call(
        update_kernel,
        grid=(half // blk,),
        out_shape=jax.ShapeDtypeStruct((half, width), f32),
        in_specs=[
            pl.BlockSpec((blk, 2 * slots), lambda i: (i, 0)),
            pl.BlockSpec((2 * slots, wide), lambda i: (0, 0)),
            pl.BlockSpec((blk, 1), lambda i: (i, 0)),
            pl.BlockSpec((1, width), lambda i: (0, 0)),
        ],
        out_specs=pl.BlockSpec((blk, width), lambda i: (i, 0)),
        compiler_params=pltpu.CompilerParams(vmem_limit_bytes=32 * 1024 * 1024),
    )(ht, rec, rfac, cfac)
    return hg[None, None], update[None], row_new, col_new


def solution(mesh):
    in_specs = (
        P("replica", "expert", None),
        P("replica", "expert", None),
        P("replica", "expert", None, "mp"),
        P("expert", "mp", None),
        P("expert", ("mp", "replica")),
        P("expert", None),
    )
    out_specs = (
        P("replica", "expert", None, "mp"),
        P("expert", ("mp", "replica"), None),
        P("expert", ("mp", "replica")),
        P("expert", None),
    )
    n = mesh.shape["expert"]
    whole_tiles = 48 * 4 // n % 16 == 0
    body = fused if whole_tiles and mesh.shape["mp"] == 4 and mesh.shape["replica"] == 2 else on_device
    return jax.shard_map(
        body, mesh=mesh, in_specs=in_specs, out_specs=out_specs, check_vma=False
    )
```

```python
import functools

import jax
import jax.numpy as jnp
from jax import lax
from jax.experimental import pallas as pl
from jax.experimental.pallas import tpu as pltpu
from jax.sharding import PartitionSpec as P

FF = 6144
EXP_DEV = 1


decay_rate = 0.8
clip_limit = 1.0
tiny_square = 1e-30


def on_device(grad_out, route, hidden_act, out_weight, row_state, col_state):
    n_expert = lax.axis_size("expert")
    tok_count = grad_out.shape[1]
    width = grad_out.shape[2]
    experts = EXP_DEV * n_expert
    capacity = 3 * tok_count // (2 * experts)
    tokens = grad_out[0]
    expert_ids = route[0, :, 0]
    onehot = (expert_ids[:, None] == jnp.arange(experts, dtype=jnp.int32)[None, :]).astype(
        jnp.float32
    )
    row_iota = lax.broadcasted_iota(jnp.int32, (tok_count, tok_count), 0)
    col_iota = lax.broadcasted_iota(jnp.int32, (tok_count, tok_count), 1)
    earlier = (row_iota > col_iota).astype(jnp.float32)
    position = jnp.sum(
        jnp.dot(earlier, onehot, preferred_element_type=jnp.float32) * onehot, axis=1
    ).astype(jnp.int32)
    slot_index = expert_ids * capacity + position
    dispatch = (
        slot_index[None, :] == jnp.arange(experts * capacity, dtype=jnp.int32)[:, None]
    ).astype(jnp.bfloat16)
    outgoing = jnp.dot(dispatch, tokens, preferred_element_type=jnp.float32).astype(jnp.bfloat16)
    outgoing = outgoing.reshape(n_expert, EXP_DEV * capacity, width)
    arrived = lax.all_to_all(outgoing, "expert", split_axis=0, concat_axis=0, tiled=True)
    arrived = arrived.reshape(n_expert, EXP_DEV, capacity, width).transpose(1, 0, 2, 3)
    arrived = arrived.reshape(EXP_DEV, n_expert * capacity, width)
    hidden = hidden_act[0]
    hidden_grad = jnp.einsum(
        "esd,efd->esf", arrived, out_weight, preferred_element_type=jnp.float32
    )
    hidden_grad = hidden_grad.astype(jnp.bfloat16)[None]
    parts = lax.all_to_all(hidden, "replica", split_axis=2, concat_axis=1, tiled=True)
    grad = jnp.einsum(
        "esf,esd->efd",
        parts,
        lax.all_gather(arrived, "replica", axis=1, tiled=True),
        preferred_element_type=jnp.float32,
    )
    squares = grad * grad + tiny_square
    row_new = decay_rate * row_state + (1.0 - decay_rate) * jnp.mean(squares, axis=2)
    col_part = jnp.sum(squares, axis=1)
    row_part = jnp.sum(row_new, axis=1)
    weighted = jnp.sum(grad * grad / row_new[:, :, None], axis=1)
    col_total, weighted_total, row_total = lax.psum(
        (col_part, weighted, row_part), ("mp", "replica")
    )
    col_new = decay_rate * col_state + (1.0 - decay_rate) * col_total / FF
    row_mean = row_total / FF
    raw_step = grad / jnp.sqrt(row_new[:, :, None] * col_new[:, None, :] / row_mean[:, None, None])
    update_sq = row_mean * jnp.sum(weighted_total / col_new, axis=1)
    update_rms = jnp.sqrt(update_sq / (FF * width))
    update = raw_step / jnp.maximum(1.0, update_rms / clip_limit)[:, None, None]
    return (hidden_grad, update, row_new, col_new)


MESH = pl.DeviceIdType.MESH
CH = 512
REM = 128


def exchange_kernel(
    n, cap, tok_ref, ids_ref, hid_ref, w_hbm, row_ref, col_ref,
    hg_ref, rownew_ref, colnew_ref, cfac_ref, rfac_ref, hs_hbm, rec_hbm,
    outb, zb, parts, hs, w, st, rowcol, colst, w_sem, loc_sem, send_sem, recv_sem,
):
    e = lax.axis_index("expert")
    m = lax.axis_index("mp")
    r = lax.axis_index("replica")
    width = tok_ref.shape[0]
    slots = n * cap
    half = hs.shape[1]
    rem = width - 4 * CH
    f32 = jnp.float32

    w_copy = pltpu.make_async_copy(w_hbm, w, w_sem)
    w_copy.start()

    def across(d):
        m2 = m + (1 - 2 * (m % 2)) * (d % 2)
        m2 = m2 + (2 - 4 * (m // 2)) * ((d // 2) % 2)
        r2 = r + (1 - 2 * r) * (d // 4)
        return (e, m2, r2)

    def along(k):
        return (lax.rem(e + k, n), m, r)

    barrier = pltpu.get_barrier_semaphore()
    for d in range(1, 8):
        pl.semaphore_signal(barrier, inc=1, device_id=across(d), device_id_type=MESH)
    for k in range(1, n):
        pl.semaphore_signal(barrier, inc=1, device_id=along(k), device_id_type=MESH)

    tc = tok_ref.shape[1]
    nt = (((1,), (1,)), ((), ()))
    ids_t = jnp.broadcast_to(ids_ref[...].astype(f32), (tc, tc))
    ids = ids_t.T
    p_i = lax.broadcasted_iota(jnp.int32, (tc, tc), 0)
    q_i = lax.broadcasted_iota(jnp.int32, (tc, tc), 1)
    before = jnp.where((p_i < q_i) & (ids == ids_t), 1.0, 0.0)
    slot = ids_t[0:1, :] * cap + jnp.sum(before, axis=0, keepdims=True)
    want = lax.broadcasted_iota(jnp.int32, (slots, tc), 0).astype(f32)
    dispatch = jnp.where(want == slot, 1.0, 0.0).astype(jnp.bfloat16)
    mine = tok_ref[pl.ds(pl.multiple_of(m * CH, CH), CH), :]
    outb[:, 0:CH] = lax.dot_general(
        dispatch, mine, nt, preferred_element_type=f32
    ).astype(jnp.bfloat16)
    outb[:, CH:] = jnp.zeros((slots, REM), jnp.bfloat16)
    outb[:, CH:CH + rem] = lax.dot_general(
        dispatch, tok_ref[4 * CH:, :], nt, preferred_element_type=f32
    ).astype(jnp.bfloat16)
    pl.semaphore_wait(barrier, 7 + n - 1)

    started = []

    def send(src, dst, to):
        i = len(started)
        c = pltpu.make_async_remote_copy(
            src_ref=src, dst_ref=dst, send_sem=send_sem.at[i], recv_sem=recv_sem.at[i],
            device_id=to, device_id_type=MESH,
        )
        c.start()
        started.append(c)
        return c

    def rows_of(k, base=0):
        return pl.ds(pl.multiple_of(base + lax.rem(e - k + n, n) * cap, 16), cap)

    own = rows_of(0)
    zc = [None]
    for k in range(1, n):
        there = pl.ds(pl.multiple_of(lax.rem(e + k, n) * cap, 16), cap)
        zc.append(send(outb.at[there, :], zb.at[own, :], along(k)))
    zb[own, :] = outb[own, :]
    other_half = pl.ds(pl.multiple_of((1 - r) * half, 128), half)
    own_half = pl.ds(pl.multiple_of(r * half, 128), half)
    xc, hc, yo, co = [], [], [], []
    for k in range(n):
        if k:
            zc[k].wait_recv()
        a, b = rows_of(k), rows_of(k, slots)
        xc.append(send(zb.at[a, :], zb.at[b, :], across(4)))
        yo.append(send(zb.at[a, 0:CH], parts.at[m, a, :], across(2)))
        co.append(send(zb.at[a, 0:CH], parts.at[m, a, :], across(1)))
    for k in range(n):
        piece = pl.ds(k * cap, cap)
        there = pl.ds(slots + k * cap, cap)
        hc.append(send(hid_ref.at[piece, other_half], hs.at[there, :], across(4)))
    m_y = across(2)[1]
    parts[m, 0:slots, :] = zb[0:slots, 0:CH]
    hs[0:slots, :] = hid_ref[:, own_half]
    fo, yx, cx, fx = [], [], [], []
    for k in range(n):
        yo[k].wait_recv()
        a = rows_of(k)
        fo.append(send(parts.at[m_y, a, :], parts.at[m_y, a, :], across(1)))
    for k in range(n):
        xc[k].wait_recv()
        b = rows_of(k, slots)
        yx.append(send(zb.at[b, 0:CH], parts.at[m, b, :], across(2)))
        cx.append(send(zb.at[b, 0:CH], parts.at[m, b, :], across(1)))
    for k in range(n):
        co[k].wait_recv()
        fo[k].wait_recv()
    w_copy.wait()

    def hidden_tile(t):
        f = pl.ds(pl.multiple_of(t * 256, 256), 256)
        acc = jnp.dot(
            zb[0:slots, CH:CH + rem], w[4 * CH:, f], preferred_element_type=f32
        )
        for c in range(4):
            acc += jnp.dot(
                parts[c, 0:slots, :], w[c * CH:(c + 1) * CH, f], preferred_element_type=f32
            )
        hg_ref[:, f] = acc.astype(jnp.bfloat16)

    tiles = hg_ref.shape[1] // 256
    for k in range(n):
        lo, hi = tiles * k // n, tiles * (k + 1) // n

        def some(t, carry):
            hidden_tile(t)
            return carry

        lax.fori_loop(lo, hi, some, 0)
        yx[k].wait_recv()
        b = rows_of(k, slots)
        fx.append(send(parts.at[m_y, b, :], parts.at[m_y, b, :], across(1)))
    parts[m, slots:, :] = zb[slots:, 0:CH]
    for k in range(n):
        hc[k].wait_recv()
        cx[k].wait_recv()
        fx[k].wait_recv()

    local = []
    for c in range(4):
        local.append(pltpu.make_async_copy(
            parts.at[c], rec_hbm.at[:, pl.ds(c * CH, CH)], loc_sem.at[c]))
    local.append(pltpu.make_async_copy(
        zb.at[:, pl.ds(CH, REM)], rec_hbm.at[:, pl.ds(4 * CH, REM)], loc_sem.at[4]))
    local.append(pltpu.make_async_copy(hs, hs_hbm, loc_sem.at[5]))
    for c in local:
        c.start()

    rowcol[...] = jnp.broadcast_to(row_ref[...], (128, half)).T
    blk = 128

    def block(t, carry):
        total, cols, weights = carry
        i = pl.ds(pl.multiple_of(t * blk, blk), blk)
        h = hs[:, i].T
        gg = []
        for c in range(5):
            rhs = parts[c] if c < 4 else zb[:, CH:CH + REM]
            g = jnp.dot(h, rhs, preferred_element_type=f32)
            gg.append(g * g)
        rs = sum(jnp.sum(x, axis=1, keepdims=True) for x in gg)
        mean = rs / width + tiny_square
        new = decay_rate * rowcol[i, 0:1] + (1.0 - decay_rate) * mean
        rowcol[i, :] = jnp.broadcast_to(new, (blk, 128))
        inv = 1.0 / new
        total = total + jnp.sum(new, axis=0, keepdims=True)
        cols = tuple(
            a + jnp.sum(x, axis=0, keepdims=True) for a, x in zip(cols, gg))
        weights = tuple(
            a + jnp.sum(x * inv, axis=0, keepdims=True) for a, x in zip(weights, gg))
        return total, cols, weights

    zero = tuple(jnp.zeros((1, CH if c < 4 else REM), f32) for c in range(5))
    total, cols, weights = lax.fori_loop(
        0, half // blk, block, (jnp.zeros((1, 1), f32), zero, zero))
    me = m * 2 + r
    cols = [x + half * tiny_square for x in cols]
    for j in range(17):
        c, o = j // 4, (j % 4) * 128
        st[me, j:j + 1, :] = cols[c][:, o:o + 128]
        st[me, 24 + j:25 + j, :] = weights[c][:, o:o + 128]
    st[me, 17:24, :] = jnp.zeros((7, 128), f32)
    st[me, 41:48, :] = jnp.broadcast_to(total, (7, 128))
    sc = [send(st.at[me], st.at[me], across(d)) for d in range(1, 8)]
    row_new = rowcol[...].T[0:1, :]
    rownew_ref[...] = row_new
    rfac_ref[...] = lax.rsqrt(row_new)
    colst[...] = jnp.ones((24, 128), f32)
    for j in range(17):
        hi = min(width, (j + 1) * 128)
        colst[j:j + 1, 0:hi - j * 128] = col_ref[:, j * 128:hi]
    for c in sc:
        c.wait_recv()
    tot = st[0]
    for j in range(1, 8):
        tot = tot + st[j]

    col_new = decay_rate * colst[...] + (1.0 - decay_rate) * (tot[0:24] / FF)
    row_mean = tot[47:48, 0:1] / FF
    weighted = jnp.where(lax.broadcasted_iota(jnp.int32, (24, 128), 0) < 17, tot[24:48], 0.0)
    ratio = jnp.sum(weighted / col_new, axis=0, keepdims=True)
    ratio = jnp.sum(ratio, axis=1, keepdims=True)
    rms = jnp.sqrt(row_mean * ratio / (FF * width))
    scale = jnp.sqrt(row_mean) / jnp.maximum(1.0, rms / clip_limit)
    cfac = lax.rsqrt(col_new) * scale
    cfac = jnp.concatenate([cfac, jnp.zeros((104, 128), f32)], axis=0).T
    for j in range(17):
        hi = min(width, (j + 1) * 128)
        colnew_ref[:, j * 128:hi] = col_new[j:j + 1, 0:hi - j * 128]
        cfac_ref[j * 128:hi, :] = cfac[0:hi - j * 128, j:j + 1]
    for c in started:
        c.wait_send()
    for c in local:
        c.wait()


def update_kernel(hs_ref, rec_ref, rfac_ref, cfac_ref, out_ref):
    g = lax.dot_general(
        rec_ref[...], hs_ref[...], (((0,), (0,)), ((), ())), preferred_element_type=jnp.float32
    )
    out_ref[...] = ((g * rfac_ref[...]) * cfac_ref[...])[0:out_ref.shape[0], :]


def fused(grad_out, route, hidden_act, out_weight, row_state, col_state):
    n = lax.axis_size("expert")
    tok_count, width = grad_out.shape[1:]
    cap = 3 * tok_count // (2 * n)
    slots = n * cap
    ff = hidden_act.shape[3]
    half = ff // 2
    bf16, f32 = jnp.bfloat16, jnp.float32
    vmem = pl.BlockSpec(memory_space=pltpu.VMEM)
    hbm = pl.BlockSpec(memory_space=pl.ANY)
    wide = 4 * CH + REM
    copies = 9 * n + n - 1 + 7
    hg, row_new, col_new, cfac, rfac, hs, rec = pl.pallas_call(
        functools.partial(exchange_kernel, n, cap),
        out_shape=[
            jax.ShapeDtypeStruct((slots, ff), bf16),
            jax.ShapeDtypeStruct((1, half), f32),
            jax.ShapeDtypeStruct((1, width), f32),
            jax.ShapeDtypeStruct((width, 1), f32),
            jax.ShapeDtypeStruct((1, half), f32),
            jax.ShapeDtypeStruct((2 * slots, half), bf16),
            jax.ShapeDtypeStruct((2 * slots, wide), bf16),
        ],
        in_specs=[vmem, vmem, vmem, hbm, vmem, vmem],
        out_specs=[vmem] * 5 + [hbm] * 2,
        scratch_shapes=[
            pltpu.VMEM((slots, CH + REM), bf16),
            pltpu.VMEM((2 * slots, CH + REM), bf16),
            pltpu.VMEM((4, 2 * slots, CH), bf16),
            pltpu.VMEM((2 * slots, half), bf16),
            pltpu.VMEM((width, ff), bf16),
            pltpu.VMEM((8, 48, 128), f32),
            pltpu.VMEM((half, 128), f32),
            pltpu.VMEM((24, 128), f32),
            pltpu.SemaphoreType.DMA,
            pltpu.SemaphoreType.DMA((6,)),
            pltpu.SemaphoreType.DMA((copies,)),
            pltpu.SemaphoreType.DMA((copies,)),
        ],
        compiler_params=pltpu.CompilerParams(
            collective_id=0, has_side_effects=True, vmem_limit_bytes=58 * 1024 * 1024
        ),
    )(
        grad_out[0].T, route[0].T, hidden_act[0, 0], out_weight[0].T, row_state, col_state
    )
    blk = 256
    update = pl.pallas_call(
        update_kernel,
        grid=(pl.cdiv(width, blk),),
        out_shape=jax.ShapeDtypeStruct((width, half), f32),
        in_specs=[
            pl.BlockSpec((2 * slots, half), lambda i: (0, 0)),
            pl.BlockSpec((2 * slots, blk), lambda i: (0, i)),
            pl.BlockSpec((1, half), lambda i: (0, 0)),
            pl.BlockSpec((blk, 1), lambda i: (i, 0)),
        ],
        out_specs=pl.BlockSpec((blk, half), lambda i: (i, 0)),
        compiler_params=pltpu.CompilerParams(vmem_limit_bytes=58 * 1024 * 1024),
    )(hs, rec, rfac, cfac).T
    return hg[None, None], update[None], row_new, col_new


def solution(mesh):
    in_specs = (
        P("replica", "expert", None),
        P("replica", "expert", None),
        P("replica", "expert", None, "mp"),
        P("expert", "mp", None),
        P("expert", ("mp", "replica")),
        P("expert", None),
    )
    out_specs = (
        P("replica", "expert", None, "mp"),
        P("expert", ("mp", "replica"), None),
        P("expert", ("mp", "replica")),
        P("expert", None),
    )
    n = mesh.shape["expert"]
    whole_tiles = 48 * 4 // n % 16 == 0
    body = fused if whole_tiles and mesh.shape["mp"] == 4 and mesh.shape["replica"] == 2 else on_device
    return jax.shard_map(
        body, mesh=mesh, in_specs=in_specs, out_specs=out_specs, check_vma=False
    )
```

```python
import functools

import jax
import jax.numpy as jnp
from jax import lax
from jax.experimental import pallas as pl
from jax.experimental.pallas import tpu as pltpu
from jax.sharding import PartitionSpec as P

FF = 6144
EXP_DEV = 1


decay_rate = 0.8
clip_limit = 1.0
tiny_square = 1e-30


def on_device(grad_out, route, hidden_act, out_weight, row_state, col_state):
    n_expert = lax.axis_size("expert")
    tok_count = grad_out.shape[1]
    width = grad_out.shape[2]
    experts = EXP_DEV * n_expert
    capacity = 3 * tok_count // (2 * experts)
    tokens = grad_out[0]
    expert_ids = route[0, :, 0]
    onehot = (expert_ids[:, None] == jnp.arange(experts, dtype=jnp.int32)[None, :]).astype(
        jnp.float32
    )
    row_iota = lax.broadcasted_iota(jnp.int32, (tok_count, tok_count), 0)
    col_iota = lax.broadcasted_iota(jnp.int32, (tok_count, tok_count), 1)
    earlier = (row_iota > col_iota).astype(jnp.float32)
    position = jnp.sum(
        jnp.dot(earlier, onehot, preferred_element_type=jnp.float32) * onehot, axis=1
    ).astype(jnp.int32)
    slot_index = expert_ids * capacity + position
    dispatch = (
        slot_index[None, :] == jnp.arange(experts * capacity, dtype=jnp.int32)[:, None]
    ).astype(jnp.bfloat16)
    outgoing = jnp.dot(dispatch, tokens, preferred_element_type=jnp.float32).astype(jnp.bfloat16)
    outgoing = outgoing.reshape(n_expert, EXP_DEV * capacity, width)
    arrived = lax.all_to_all(outgoing, "expert", split_axis=0, concat_axis=0, tiled=True)
    arrived = arrived.reshape(n_expert, EXP_DEV, capacity, width).transpose(1, 0, 2, 3)
    arrived = arrived.reshape(EXP_DEV, n_expert * capacity, width)
    hidden = hidden_act[0]
    hidden_grad = jnp.einsum(
        "esd,efd->esf", arrived, out_weight, preferred_element_type=jnp.float32
    )
    hidden_grad = hidden_grad.astype(jnp.bfloat16)[None]
    parts = lax.all_to_all(hidden, "replica", split_axis=2, concat_axis=1, tiled=True)
    grad = jnp.einsum(
        "esf,esd->efd",
        parts,
        lax.all_gather(arrived, "replica", axis=1, tiled=True),
        preferred_element_type=jnp.float32,
    )
    squares = grad * grad + tiny_square
    row_new = decay_rate * row_state + (1.0 - decay_rate) * jnp.mean(squares, axis=2)
    col_part = jnp.sum(squares, axis=1)
    row_part = jnp.sum(row_new, axis=1)
    weighted = jnp.sum(grad * grad / row_new[:, :, None], axis=1)
    col_total, weighted_total, row_total = lax.psum(
        (col_part, weighted, row_part), ("mp", "replica")
    )
    col_new = decay_rate * col_state + (1.0 - decay_rate) * col_total / FF
    row_mean = row_total / FF
    raw_step = grad / jnp.sqrt(row_new[:, :, None] * col_new[:, None, :] / row_mean[:, None, None])
    update_sq = row_mean * jnp.sum(weighted_total / col_new, axis=1)
    update_rms = jnp.sqrt(update_sq / (FF * width))
    update = raw_step / jnp.maximum(1.0, update_rms / clip_limit)[:, None, None]
    return (hidden_grad, update, row_new, col_new)


MESH = pl.DeviceIdType.MESH
CH = 512
REM = 128


def exchange_kernel(
    n, cap, tok_ref, ids_ref, hid_ref, w_hbm, row_ref, col_ref,
    hg_ref, rownew_ref, colnew_ref, cfac_ref, rfac_ref, hs_hbm, rec_hbm,
    outb, zb, parts, hs, w, st, rowcol, colst, w_sem, loc_sem, send_sem, recv_sem,
):
    e = lax.axis_index("expert")
    m = lax.axis_index("mp")
    r = lax.axis_index("replica")
    width = tok_ref.shape[0]
    slots = n * cap
    half = hs.shape[1]
    rem = width - 4 * CH
    f32 = jnp.float32

    w_copy = pltpu.make_async_copy(w_hbm, w, w_sem)
    w_copy.start()

    def across(d):
        m2 = m + (1 - 2 * (m % 2)) * (d % 2)
        m2 = m2 + (2 - 4 * (m // 2)) * ((d // 2) % 2)
        r2 = r + (1 - 2 * r) * (d // 4)
        return (e, m2, r2)

    def along(k):
        return (lax.rem(e + k, n), m, r)

    barrier = pltpu.get_barrier_semaphore()
    for d in range(1, 8):
        pl.semaphore_signal(barrier, inc=1, device_id=across(d), device_id_type=MESH)
    for k in range(1, n):
        pl.semaphore_signal(barrier, inc=1, device_id=along(k), device_id_type=MESH)

    tc = tok_ref.shape[1]
    nt = (((1,), (1,)), ((), ()))
    ids_t = jnp.broadcast_to(ids_ref[...].astype(f32), (tc, tc))
    ids = ids_t.T
    p_i = lax.broadcasted_iota(jnp.int32, (tc, tc), 0)
    q_i = lax.broadcasted_iota(jnp.int32, (tc, tc), 1)
    before = jnp.where((p_i < q_i) & (ids == ids_t), 1.0, 0.0)
    slot = ids_t[0:1, :] * cap + jnp.sum(before, axis=0, keepdims=True)
    want = lax.broadcasted_iota(jnp.int32, (slots, tc), 0).astype(f32)
    dispatch = jnp.where(want == slot, 1.0, 0.0).astype(jnp.bfloat16)
    mine = tok_ref[pl.ds(pl.multiple_of(m * CH, CH), CH), :]
    outb[:, 0:CH] = lax.dot_general(
        dispatch, mine, nt, preferred_element_type=f32
    ).astype(jnp.bfloat16)
    outb[:, CH:] = jnp.zeros((slots, REM), jnp.bfloat16)
    outb[:, CH:CH + rem] = lax.dot_general(
        dispatch, tok_ref[4 * CH:, :], nt, preferred_element_type=f32
    ).astype(jnp.bfloat16)
    pl.semaphore_wait(barrier, 7 + n - 1)

    started = []

    def send(src, dst, to):
        i = len(started)
        c = pltpu.make_async_remote_copy(
            src_ref=src, dst_ref=dst, send_sem=send_sem.at[i], recv_sem=recv_sem.at[i],
            device_id=to, device_id_type=MESH,
        )
        c.start()
        started.append(c)
        return c

    def rows_of(k, base=0):
        return pl.ds(pl.multiple_of(base + lax.rem(e - k + n, n) * cap, 16), cap)

    own = rows_of(0)
    zc = [None]
    for k in range(1, n):
        there = pl.ds(pl.multiple_of(lax.rem(e + k, n) * cap, 16), cap)
        zc.append(send(outb.at[there, :], zb.at[own, :], along(k)))
    zb[own, :] = outb[own, :]
    other_half = pl.ds(pl.multiple_of((1 - r) * half, 128), half)
    own_half = pl.ds(pl.multiple_of(r * half, 128), half)
    xc, hc, yo, co = [], [], [], []
    for k in range(n):
        if k:
            zc[k].wait_recv()
        a, b = rows_of(k), rows_of(k, slots)
        xc.append(send(zb.at[a, :], zb.at[b, :], across(4)))
        yo.append(send(zb.at[a, 0:CH], parts.at[m, a, :], across(2)))
        co.append(send(zb.at[a, 0:CH], parts.at[m, a, :], across(1)))
    for k in range(n):
        piece = pl.ds(k * cap, cap)
        there = pl.ds(slots + k * cap, cap)
        hc.append(send(hid_ref.at[piece, other_half], hs.at[there, :], across(4)))
    m_y = across(2)[1]
    parts[m, 0:slots, :] = zb[0:slots, 0:CH]
    hs[0:slots, :] = hid_ref[:, own_half]
    fo, yx, cx, fx = [], [], [], []
    for k in range(n):
        yo[k].wait_recv()
        a = rows_of(k)
        fo.append(send(parts.at[m_y, a, :], parts.at[m_y, a, :], across(1)))
    for k in range(n):
        xc[k].wait_recv()
        b = rows_of(k, slots)
        yx.append(send(zb.at[b, 0:CH], parts.at[m, b, :], across(2)))
        cx.append(send(zb.at[b, 0:CH], parts.at[m, b, :], across(1)))
    for k in range(n):
        co[k].wait_recv()
        fo[k].wait_recv()
    w_copy.wait()

    def hidden_tile(t):
        f = pl.ds(pl.multiple_of(t * 256, 256), 256)
        acc = jnp.dot(
            zb[0:slots, CH:CH + rem], w[4 * CH:, f], preferred_element_type=f32
        )
        for c in range(4):
            acc += jnp.dot(
                parts[c, 0:slots, :], w[c * CH:(c + 1) * CH, f], preferred_element_type=f32
            )
        hg_ref[:, f] = acc.astype(jnp.bfloat16)

    tiles = hg_ref.shape[1] // 256
    for k in range(n):
        lo, hi = tiles * k // n, tiles * (k + 1) // n

        def some(t, carry):
            hidden_tile(t)
            return carry

        lax.fori_loop(lo, hi, some, 0)
        yx[k].wait_recv()
        b = rows_of(k, slots)
        fx.append(send(parts.at[m_y, b, :], parts.at[m_y, b, :], across(1)))
    parts[m, slots:, :] = zb[slots:, 0:CH]
    for k in range(n):
        hc[k].wait_recv()
        cx[k].wait_recv()
        fx[k].wait_recv()

    local = []
    for c in range(4):
        local.append(pltpu.make_async_copy(
            parts.at[c], rec_hbm.at[:, pl.ds(c * CH, CH)], loc_sem.at[c]))
    local.append(pltpu.make_async_copy(
        zb.at[:, pl.ds(CH, REM)], rec_hbm.at[:, pl.ds(4 * CH, REM)], loc_sem.at[4]))
    local.append(pltpu.make_async_copy(hs, hs_hbm, loc_sem.at[5]))
    for c in local:
        c.start()

    rowcol[...] = jnp.broadcast_to(row_ref[...], (128, half)).T
    blk = 128

    def block(t, carry):
        total, cols, weights = carry
        i = pl.ds(pl.multiple_of(t * blk, blk), blk)
        h = hs[:, i].T
        gg = []
        for c in range(5):
            rhs = parts[c] if c < 4 else zb[:, CH:CH + REM]
            g = jnp.dot(h, rhs, preferred_element_type=f32)
            gg.append(g * g)
        lanes = sum(x[:, o:o + 128] for x in gg for o in range(0, x.shape[1], 128))
        rs = jnp.sum(lanes, axis=1, keepdims=True)
        mean = rs / width + tiny_square
        new = decay_rate * rowcol[i, 0:1] + (1.0 - decay_rate) * mean
        rowcol[i, :] = jnp.broadcast_to(new, (blk, 128))
        inv = 1.0 / new
        total = total + jnp.sum(new, axis=0, keepdims=True)
        cols = tuple(
            a + jnp.sum(x.reshape(blk // 8, 8, -1), axis=0) for a, x in zip(cols, gg))
        weights = tuple(
            a + jnp.sum((x * inv).reshape(blk // 8, 8, -1), axis=0) for a, x in zip(weights, gg))
        return total, cols, weights

    zero = tuple(jnp.zeros((8, CH if c < 4 else REM), f32) for c in range(5))
    total, cols, weights = lax.fori_loop(
        0, half // blk, block, (jnp.zeros((1, 1), f32), zero, zero))
    me = m * 2 + r
    cols = [jnp.sum(x, axis=0, keepdims=True) + half * tiny_square for x in cols]
    weights = [jnp.sum(x, axis=0, keepdims=True) for x in weights]
    for j in range(17):
        c, o = j // 4, (j % 4) * 128
        st[me, j:j + 1, :] = cols[c][:, o:o + 128]
        st[me, 24 + j:25 + j, :] = weights[c][:, o:o + 128]
    st[me, 17:24, :] = jnp.zeros((7, 128), f32)
    st[me, 41:48, :] = jnp.broadcast_to(total, (7, 128))
    sc = [send(st.at[me], st.at[me], across(d)) for d in range(1, 8)]
    row_new = rowcol[...].T[0:1, :]
    rownew_ref[...] = row_new
    rfac_ref[...] = lax.rsqrt(row_new)
    colst[...] = jnp.ones((24, 128), f32)
    for j in range(17):
        hi = min(width, (j + 1) * 128)
        colst[j:j + 1, 0:hi - j * 128] = col_ref[:, j * 128:hi]
    for c in sc:
        c.wait_recv()
    tot = st[0]
    for j in range(1, 8):
        tot = tot + st[j]

    col_new = decay_rate * colst[...] + (1.0 - decay_rate) * (tot[0:24] / FF)
    row_mean = tot[47:48, 0:1] / FF
    weighted = jnp.where(lax.broadcasted_iota(jnp.int32, (24, 128), 0) < 17, tot[24:48], 0.0)
    ratio = jnp.sum(weighted / col_new, axis=0, keepdims=True)
    ratio = jnp.sum(ratio, axis=1, keepdims=True)
    rms = jnp.sqrt(row_mean * ratio / (FF * width))
    scale = jnp.sqrt(row_mean) / jnp.maximum(1.0, rms / clip_limit)
    cfac = lax.rsqrt(col_new) * scale
    cfac = jnp.concatenate([cfac, jnp.zeros((104, 128), f32)], axis=0).T
    for j in range(17):
        hi = min(width, (j + 1) * 128)
        colnew_ref[:, j * 128:hi] = col_new[j:j + 1, 0:hi - j * 128]
        cfac_ref[j * 128:hi, :] = cfac[0:hi - j * 128, j:j + 1]
    for c in started:
        c.wait_send()
    for c in local:
        c.wait()


def update_kernel(
    hs_ref, rec_ref, rfac_ref, cfac_ref, hg_ref, row_ref, col_ref,
    out_ref, hg_out, row_out, col_out,
):
    hg_out[...] = hg_ref[...]
    row_out[...] = row_ref[...]
    col_out[...] = col_ref[...]
    g = lax.dot_general(
        rec_ref[...], hs_ref[...], (((0,), (0,)), ((), ())), preferred_element_type=jnp.float32
    )
    out_ref[...] = ((g * rfac_ref[...]) * cfac_ref[...])[0:out_ref.shape[0], :]


def fused(grad_out, route, hidden_act, out_weight, row_state, col_state):
    n = lax.axis_size("expert")
    tok_count, width = grad_out.shape[1:]
    cap = 3 * tok_count // (2 * n)
    slots = n * cap
    ff = hidden_act.shape[3]
    half = ff // 2
    bf16, f32 = jnp.bfloat16, jnp.float32
    vmem = pl.BlockSpec(memory_space=pltpu.VMEM)
    hbm = pl.BlockSpec(memory_space=pl.ANY)
    wide = 4 * CH + REM
    copies = 9 * n + n - 1 + 7
    hg, row_new, col_new, cfac, rfac, hs, rec = pl.pallas_call(
        functools.partial(exchange_kernel, n, cap),
        out_shape=[
            jax.ShapeDtypeStruct((slots, ff), bf16),
            jax.ShapeDtypeStruct((1, half), f32),
            jax.ShapeDtypeStruct((1, width), f32),
            jax.ShapeDtypeStruct((width, 1), f32),
            jax.ShapeDtypeStruct((1, half), f32),
            jax.ShapeDtypeStruct((2 * slots, half), bf16),
            jax.ShapeDtypeStruct((2 * slots, wide), bf16),
        ],
        in_specs=[vmem, vmem, vmem, hbm, vmem, vmem],
        out_specs=[vmem] * 5 + [hbm] * 2,
        scratch_shapes=[
            pltpu.VMEM((slots, CH + REM), bf16),
            pltpu.VMEM((2 * slots, CH + REM), bf16),
            pltpu.VMEM((4, 2 * slots, CH), bf16),
            pltpu.VMEM((2 * slots, half), bf16),
            pltpu.VMEM((width, ff), bf16),
            pltpu.VMEM((8, 48, 128), f32),
            pltpu.VMEM((half, 128), f32),
            pltpu.VMEM((24, 128), f32),
            pltpu.SemaphoreType.DMA,
            pltpu.SemaphoreType.DMA((6,)),
            pltpu.SemaphoreType.DMA((copies,)),
            pltpu.SemaphoreType.DMA((copies,)),
        ],
        compiler_params=pltpu.CompilerParams(
            collective_id=0, has_side_effects=True, vmem_limit_bytes=58 * 1024 * 1024
        ),
    )(
        grad_out[0].T, route[0].T, hidden_act[0, 0], out_weight[0].T, row_state, col_state
    )
    blk = 1024
    steps = pl.cdiv(width, blk)
    update, hg, row_new, col_new = pl.pallas_call(
        update_kernel,
        grid=(steps,),
        out_shape=[
            jax.ShapeDtypeStruct((width, half), f32),
            jax.ShapeDtypeStruct((slots, ff), bf16),
            jax.ShapeDtypeStruct((1, half), f32),
            jax.ShapeDtypeStruct((1, width), f32),
        ],
        in_specs=[
            pl.BlockSpec((2 * slots, half), lambda i: (0, 0)),
            pl.BlockSpec((2 * slots, blk), lambda i: (0, i)),
            pl.BlockSpec((1, half), lambda i: (0, 0)),
            pl.BlockSpec((blk, 1), lambda i: (i, 0)),
            pl.BlockSpec((slots // steps, ff), lambda i: (i, 0)),
            pl.BlockSpec((1, half), lambda i: (0, 0)),
            pl.BlockSpec((1, width), lambda i: (0, 0)),
        ],
        out_specs=[
            pl.BlockSpec((blk, half), lambda i: (i, 0)),
            pl.BlockSpec((slots // steps, ff), lambda i: (i, 0)),
            pl.BlockSpec((1, half), lambda i: (0, 0)),
            pl.BlockSpec((1, width), lambda i: (0, 0)),
        ],
        compiler_params=pltpu.CompilerParams(vmem_limit_bytes=58 * 1024 * 1024),
    )(hs, rec, rfac, cfac, hg, row_new, col_new)
    return hg[None, None], update.T[None], row_new, col_new


def solution(mesh):
    in_specs = (
        P("replica", "expert", None),
        P("replica", "expert", None),
        P("replica", "expert", None, "mp"),
        P("expert", "mp", None),
        P("expert", ("mp", "replica")),
        P("expert", None),
    )
    out_specs = (
        P("replica", "expert", None, "mp"),
        P("expert", ("mp", "replica"), None),
        P("expert", ("mp", "replica")),
        P("expert", None),
    )
    n = mesh.shape["expert"]
    whole_tiles = 48 * 4 // n % 16 == 0
    body = fused if whole_tiles and mesh.shape["mp"] == 4 and mesh.shape["replica"] == 2 else on_device
    return jax.shard_map(
        body, mesh=mesh, in_specs=in_specs, out_specs=out_specs, check_vma=False
    )
```

```python
import functools

import jax
import jax.numpy as jnp
from jax import lax
from jax.experimental import pallas as pl
from jax.experimental.pallas import tpu as pltpu
from jax.sharding import PartitionSpec as P

FF = 6144
EXP_DEV = 1


decay_rate = 0.8
clip_limit = 1.0
tiny_square = 1e-30


def on_device(grad_out, route, hidden_act, out_weight, row_state, col_state):
    n_expert = lax.axis_size("expert")
    tok_count = grad_out.shape[1]
    width = grad_out.shape[2]
    experts = EXP_DEV * n_expert
    capacity = 3 * tok_count // (2 * experts)
    tokens = grad_out[0]
    expert_ids = route[0, :, 0]
    onehot = (expert_ids[:, None] == jnp.arange(experts, dtype=jnp.int32)[None, :]).astype(
        jnp.float32
    )
    row_iota = lax.broadcasted_iota(jnp.int32, (tok_count, tok_count), 0)
    col_iota = lax.broadcasted_iota(jnp.int32, (tok_count, tok_count), 1)
    earlier = (row_iota > col_iota).astype(jnp.float32)
    position = jnp.sum(
        jnp.dot(earlier, onehot, preferred_element_type=jnp.float32) * onehot, axis=1
    ).astype(jnp.int32)
    slot_index = expert_ids * capacity + position
    dispatch = (
        slot_index[None, :] == jnp.arange(experts * capacity, dtype=jnp.int32)[:, None]
    ).astype(jnp.bfloat16)
    outgoing = jnp.dot(dispatch, tokens, preferred_element_type=jnp.float32).astype(jnp.bfloat16)
    outgoing = outgoing.reshape(n_expert, EXP_DEV * capacity, width)
    arrived = lax.all_to_all(outgoing, "expert", split_axis=0, concat_axis=0, tiled=True)
    arrived = arrived.reshape(n_expert, EXP_DEV, capacity, width).transpose(1, 0, 2, 3)
    arrived = arrived.reshape(EXP_DEV, n_expert * capacity, width)
    hidden = hidden_act[0]
    hidden_grad = jnp.einsum(
        "esd,efd->esf", arrived, out_weight, preferred_element_type=jnp.float32
    )
    hidden_grad = hidden_grad.astype(jnp.bfloat16)[None]
    parts = lax.all_to_all(hidden, "replica", split_axis=2, concat_axis=1, tiled=True)
    grad = jnp.einsum(
        "esf,esd->efd",
        parts,
        lax.all_gather(arrived, "replica", axis=1, tiled=True),
        preferred_element_type=jnp.float32,
    )
    squares = grad * grad + tiny_square
    row_new = decay_rate * row_state + (1.0 - decay_rate) * jnp.mean(squares, axis=2)
    col_part = jnp.sum(squares, axis=1)
    row_part = jnp.sum(row_new, axis=1)
    weighted = jnp.sum(grad * grad / row_new[:, :, None], axis=1)
    col_total, weighted_total, row_total = lax.psum(
        (col_part, weighted, row_part), ("mp", "replica")
    )
    col_new = decay_rate * col_state + (1.0 - decay_rate) * col_total / FF
    row_mean = row_total / FF
    raw_step = grad / jnp.sqrt(row_new[:, :, None] * col_new[:, None, :] / row_mean[:, None, None])
    update_sq = row_mean * jnp.sum(weighted_total / col_new, axis=1)
    update_rms = jnp.sqrt(update_sq / (FF * width))
    update = raw_step / jnp.maximum(1.0, update_rms / clip_limit)[:, None, None]
    return (hidden_grad, update, row_new, col_new)


MESH = pl.DeviceIdType.MESH
CH = 512
REM = 128


def exchange_kernel(
    n, cap, tok_hbm, ids_ref, hid_hbm, w_hbm, row_ref, col_ref,
    hg_hbm, rownew_ref, colnew_ref, cfac_ref, rfac_ref, hs_hbm, rec_hbm,
    outb, zb, parts, hs, w, st, rowcol, colst, tok_ref, hid_ref, hg_ref, w_sem, loc_sem, send_sem, recv_sem,
):
    e = lax.axis_index("expert")
    m = lax.axis_index("mp")
    r = lax.axis_index("replica")
    width = tok_ref.shape[0]
    slots = n * cap
    half = hs.shape[1]
    rem = width - 4 * CH
    f32 = jnp.float32

    tok_copy = pltpu.make_async_copy(tok_hbm, tok_ref, loc_sem.at[6])
    tok_copy.start()
    hid_copy = pltpu.make_async_copy(hid_hbm, hid_ref, loc_sem.at[7])
    hid_copy.start()
    w_copy = pltpu.make_async_copy(w_hbm, w, w_sem)

    def across(d):
        m2 = m + (1 - 2 * (m % 2)) * (d % 2)
        m2 = m2 + (2 - 4 * (m // 2)) * ((d // 2) % 2)
        r2 = r + (1 - 2 * r) * (d // 4)
        return (e, m2, r2)

    def along(k):
        return (lax.rem(e + k, n), m, r)

    barrier = pltpu.get_barrier_semaphore()
    for d in range(1, 8):
        pl.semaphore_signal(barrier, inc=1, device_id=across(d), device_id_type=MESH)
    for k in range(1, n):
        pl.semaphore_signal(barrier, inc=1, device_id=along(k), device_id_type=MESH)

    tc = tok_ref.shape[1]
    nt = (((1,), (1,)), ((), ()))
    ids_t = jnp.broadcast_to(ids_ref[...].astype(f32), (tc, tc))
    ids = ids_t.T
    p_i = lax.broadcasted_iota(jnp.int32, (tc, tc), 0)
    q_i = lax.broadcasted_iota(jnp.int32, (tc, tc), 1)
    before = jnp.where((p_i < q_i) & (ids == ids_t), 1.0, 0.0)
    slot = ids_t[0:1, :] * cap + jnp.sum(before, axis=0, keepdims=True)
    want = lax.broadcasted_iota(jnp.int32, (slots, tc), 0).astype(f32)
    dispatch = jnp.where(want == slot, 1.0, 0.0).astype(jnp.bfloat16)
    tok_copy.wait()
    w_copy.start()
    mine = tok_ref[pl.ds(pl.multiple_of(m * CH, CH), CH), :]
    outb[:, 0:CH] = lax.dot_general(
        dispatch, mine, nt, preferred_element_type=f32
    ).astype(jnp.bfloat16)
    outb[:, CH:] = jnp.zeros((slots, REM), jnp.bfloat16)
    outb[:, CH:CH + rem] = lax.dot_general(
        dispatch, tok_ref[4 * CH:, :], nt, preferred_element_type=f32
    ).astype(jnp.bfloat16)
    pl.semaphore_wait(barrier, 7 + n - 1)

    started = []

    def send(src, dst, to):
        i = len(started)
        c = pltpu.make_async_remote_copy(
            src_ref=src, dst_ref=dst, send_sem=send_sem.at[i], recv_sem=recv_sem.at[i],
            device_id=to, device_id_type=MESH,
        )
        c.start()
        started.append(c)
        return c

    def rows_of(k, base=0):
        return pl.ds(pl.multiple_of(base + lax.rem(e - k + n, n) * cap, 16), cap)

    own = rows_of(0)
    zc = [None]
    for k in range(1, n):
        there = pl.ds(pl.multiple_of(lax.rem(e + k, n) * cap, 16), cap)
        zc.append(send(outb.at[there, :], zb.at[own, :], along(k)))
    zb[own, :] = outb[own, :]
    other_half = pl.ds(pl.multiple_of((1 - r) * half, 128), half)
    own_half = pl.ds(pl.multiple_of(r * half, 128), half)
    xc, hc, yo, co = [], [], [], []
    for k in range(n):
        if k:
            zc[k].wait_recv()
        a, b = rows_of(k), rows_of(k, slots)
        xc.append(send(zb.at[a, :], zb.at[b, :], across(4)))
        yo.append(send(zb.at[a, 0:CH], parts.at[m, a, :], across(2)))
        co.append(send(zb.at[a, 0:CH], parts.at[m, a, :], across(1)))
    hid_copy.wait()
    for k in range(n):
        piece = pl.ds(k * cap, cap)
        there = pl.ds(slots + k * cap, cap)
        hc.append(send(hid_ref.at[piece, other_half], hs.at[there, :], across(4)))
    m_y = across(2)[1]
    parts[m, 0:slots, :] = zb[0:slots, 0:CH]
    hs[0:slots, :] = hid_ref[:, own_half]
    fo, yx, cx, fx = [], [], [], []
    for k in range(n):
        yo[k].wait_recv()
        a = rows_of(k)
        fo.append(send(parts.at[m_y, a, :], parts.at[m_y, a, :], across(1)))
    for k in range(n):
        xc[k].wait_recv()
        b = rows_of(k, slots)
        yx.append(send(zb.at[b, 0:CH], parts.at[m, b, :], across(2)))
        cx.append(send(zb.at[b, 0:CH], parts.at[m, b, :], across(1)))
    for k in range(n):
        co[k].wait_recv()
        fo[k].wait_recv()
    w_copy.wait()

    def hidden_tile(t):
        f = pl.ds(pl.multiple_of(t * 256, 256), 256)
        acc = jnp.dot(
            zb[0:slots, CH:CH + rem], w[4 * CH:, f], preferred_element_type=f32
        )
        for c in range(4):
            acc += jnp.dot(
                parts[c, 0:slots, :], w[c * CH:(c + 1) * CH, f], preferred_element_type=f32
            )
        hg_ref[:, f] = acc.astype(jnp.bfloat16)

    tiles = hg_ref.shape[1] // 256
    for k in range(n):
        lo, hi = tiles * k // n, tiles * (k + 1) // n

        def some(t, carry):
            hidden_tile(t)
            return carry

        lax.fori_loop(lo, hi, some, 0)
        yx[k].wait_recv()
        b = rows_of(k, slots)
        fx.append(send(parts.at[m_y, b, :], parts.at[m_y, b, :], across(1)))
    hg_copy = pltpu.make_async_copy(hg_ref, hg_hbm, loc_sem.at[8])
    hg_copy.start()
    parts[m, slots:, :] = zb[slots:, 0:CH]
    for k in range(n):
        hc[k].wait_recv()
        cx[k].wait_recv()
        fx[k].wait_recv()

    local = []
    for c in range(4):
        local.append(pltpu.make_async_copy(
            parts.at[c], rec_hbm.at[:, pl.ds(c * CH, CH)], loc_sem.at[c]))
    local.append(pltpu.make_async_copy(
        zb.at[:, pl.ds(CH, REM)], rec_hbm.at[:, pl.ds(4 * CH, REM)], loc_sem.at[4]))
    local.append(pltpu.make_async_copy(hs, hs_hbm, loc_sem.at[5]))
    for c in local:
        c.start()

    rowcol[...] = jnp.broadcast_to(row_ref[...], (128, half)).T
    blk = 128

    def block(t, carry):
        total, cols, weights = carry
        i = pl.ds(pl.multiple_of(t * blk, blk), blk)
        h = hs[:, i].T
        gg = []
        for c in range(5):
            rhs = parts[c] if c < 4 else zb[:, CH:CH + REM]
            g = jnp.dot(h, rhs, preferred_element_type=f32)
            gg.append(g * g)
        lanes = sum(x[:, o:o + 128] for x in gg for o in range(0, x.shape[1], 128))
        rs = jnp.sum(lanes, axis=1, keepdims=True)
        mean = rs / width + tiny_square
        new = decay_rate * rowcol[i, 0:1] + (1.0 - decay_rate) * mean
        rowcol[i, :] = jnp.broadcast_to(new, (blk, 128))
        inv = 1.0 / new
        total = total + jnp.sum(new, axis=0, keepdims=True)
        cols = tuple(
            a + jnp.sum(x.reshape(blk // 8, 8, -1), axis=0) for a, x in zip(cols, gg))
        weights = tuple(
            a + jnp.sum((x * inv).reshape(blk // 8, 8, -1), axis=0) for a, x in zip(weights, gg))
        return total, cols, weights

    zero = tuple(jnp.zeros((8, CH if c < 4 else REM), f32) for c in range(5))
    total, cols, weights = lax.fori_loop(
        0, half // blk, block, (jnp.zeros((1, 1), f32), zero, zero))
    me = m * 2 + r
    cols = [jnp.sum(x, axis=0, keepdims=True) + half * tiny_square for x in cols]
    weights = [jnp.sum(x, axis=0, keepdims=True) for x in weights]
    for j in range(17):
        c, o = j // 4, (j % 4) * 128
        st[me, j:j + 1, :] = cols[c][:, o:o + 128]
        st[me, 24 + j:25 + j, :] = weights[c][:, o:o + 128]
    st[me, 17:24, :] = jnp.zeros((7, 128), f32)
    st[me, 41:48, :] = jnp.broadcast_to(total, (7, 128))
    sc = [send(st.at[me], st.at[me], across(d)) for d in range(1, 8)]
    row_new = rowcol[...].T[0:1, :]
    rownew_ref[...] = row_new
    rfac_ref[...] = lax.rsqrt(row_new)
    colst[...] = jnp.ones((24, 128), f32)
    for j in range(17):
        hi = min(width, (j + 1) * 128)
        colst[j:j + 1, 0:hi - j * 128] = col_ref[:, j * 128:hi]
    for c in sc:
        c.wait_recv()
    tot = st[0]
    for j in range(1, 8):
        tot = tot + st[j]

    col_new = decay_rate * colst[...] + (1.0 - decay_rate) * (tot[0:24] / FF)
    row_mean = tot[47:48, 0:1] / FF
    weighted = jnp.where(lax.broadcasted_iota(jnp.int32, (24, 128), 0) < 17, tot[24:48], 0.0)
    ratio = jnp.sum(weighted / col_new, axis=0, keepdims=True)
    ratio = jnp.sum(ratio, axis=1, keepdims=True)
    rms = jnp.sqrt(row_mean * ratio / (FF * width))
    scale = jnp.sqrt(row_mean) / jnp.maximum(1.0, rms / clip_limit)
    cfac = lax.rsqrt(col_new) * scale
    cfac = jnp.concatenate([cfac, jnp.zeros((104, 128), f32)], axis=0).T
    for j in range(17):
        hi = min(width, (j + 1) * 128)
        colnew_ref[:, j * 128:hi] = col_new[j:j + 1, 0:hi - j * 128]
        cfac_ref[j * 128:hi, :] = cfac[0:hi - j * 128, j:j + 1]
    for c in started:
        c.wait_send()
    for c in local:
        c.wait()
    hg_copy.wait()


def update_kernel(
    hs_ref, rec_ref, rfac_ref, cfac_ref, hg_ref, row_ref, col_ref,
    out_ref, hg_out, row_out, col_out,
):
    hg_out[...] = hg_ref[...]
    row_out[...] = row_ref[...]
    col_out[...] = col_ref[...]
    g = lax.dot_general(
        rec_ref[...], hs_ref[...], (((0,), (0,)), ((), ())), preferred_element_type=jnp.float32
    )
    out_ref[...] = ((g * rfac_ref[...]) * cfac_ref[...])[0:out_ref.shape[0], :]


def fused(grad_out, route, hidden_act, out_weight, row_state, col_state):
    n = lax.axis_size("expert")
    tok_count, width = grad_out.shape[1:]
    cap = 3 * tok_count // (2 * n)
    slots = n * cap
    ff = hidden_act.shape[3]
    half = ff // 2
    bf16, f32 = jnp.bfloat16, jnp.float32
    vmem = pl.BlockSpec(memory_space=pltpu.VMEM)
    hbm = pl.BlockSpec(memory_space=pl.ANY)
    wide = 4 * CH + REM
    copies = 9 * n + n - 1 + 7
    hg, row_new, col_new, cfac, rfac, hs, rec = pl.pallas_call(
        functools.partial(exchange_kernel, n, cap),
        out_shape=[
            jax.ShapeDtypeStruct((slots, ff), bf16),
            jax.ShapeDtypeStruct((1, half), f32),
            jax.ShapeDtypeStruct((1, width), f32),
            jax.ShapeDtypeStruct((width, 1), f32),
            jax.ShapeDtypeStruct((1, half), f32),
            jax.ShapeDtypeStruct((2 * slots, half), bf16),
            jax.ShapeDtypeStruct((2 * slots, wide), bf16),
        ],
        in_specs=[hbm, vmem, hbm, hbm, vmem, vmem],
        out_specs=[hbm] + [vmem] * 4 + [hbm] * 2,
        scratch_shapes=[
            pltpu.VMEM((slots, CH + REM), bf16),
            pltpu.VMEM((2 * slots, CH + REM), bf16),
            pltpu.VMEM((4, 2 * slots, CH), bf16),
            pltpu.VMEM((2 * slots, half), bf16),
            pltpu.VMEM((width, ff), bf16),
            pltpu.VMEM((8, 48, 128), f32),
            pltpu.VMEM((half, 128), f32),
            pltpu.VMEM((24, 128), f32),
            pltpu.VMEM((width, tok_count), bf16),
            pltpu.VMEM((slots, ff), bf16),
            pltpu.VMEM((slots, ff), bf16),
            pltpu.SemaphoreType.DMA,
            pltpu.SemaphoreType.DMA((9,)),
            pltpu.SemaphoreType.DMA((copies,)),
            pltpu.SemaphoreType.DMA((copies,)),
        ],
        compiler_params=pltpu.CompilerParams(
            collective_id=0, has_side_effects=True, vmem_limit_bytes=58 * 1024 * 1024
        ),
    )(
        grad_out[0].T, route[0].T, hidden_act[0, 0], out_weight[0].T, row_state, col_state
    )
    blk = 1024
    steps = pl.cdiv(width, blk)
    update, hg, row_new, col_new = pl.pallas_call(
        update_kernel,
        grid=(steps,),
        out_shape=[
            jax.ShapeDtypeStruct((width, half), f32),
            jax.ShapeDtypeStruct((slots, ff), bf16),
            jax.ShapeDtypeStruct((1, half), f32),
            jax.ShapeDtypeStruct((1, width), f32),
        ],
        in_specs=[
            pl.BlockSpec((2 * slots, half), lambda i: (0, 0)),
            pl.BlockSpec((2 * slots, blk), lambda i: (0, i)),
            pl.BlockSpec((1, half), lambda i: (0, 0)),
            pl.BlockSpec((blk, 1), lambda i: (i, 0)),
            pl.BlockSpec((slots // steps, ff), lambda i: (i, 0)),
            pl.BlockSpec((1, half), lambda i: (0, 0)),
            pl.BlockSpec((1, width), lambda i: (0, 0)),
        ],
        out_specs=[
            pl.BlockSpec((blk, half), lambda i: (i, 0)),
            pl.BlockSpec((slots // steps, ff), lambda i: (i, 0)),
            pl.BlockSpec((1, half), lambda i: (0, 0)),
            pl.BlockSpec((1, width), lambda i: (0, 0)),
        ],
        compiler_params=pltpu.CompilerParams(vmem_limit_bytes=58 * 1024 * 1024),
    )(hs, rec, rfac, cfac, hg, row_new, col_new)
    return hg[None, None], update.T[None], row_new, col_new


def solution(mesh):
    in_specs = (
        P("replica", "expert", None),
        P("replica", "expert", None),
        P("replica", "expert", None, "mp"),
        P("expert", "mp", None),
        P("expert", ("mp", "replica")),
        P("expert", None),
    )
    out_specs = (
        P("replica", "expert", None, "mp"),
        P("expert", ("mp", "replica"), None),
        P("expert", ("mp", "replica")),
        P("expert", None),
    )
    n = mesh.shape["expert"]
    whole_tiles = 48 * 4 // n % 16 == 0
    body = fused if whole_tiles and mesh.shape["mp"] == 4 and mesh.shape["replica"] == 2 else on_device
    return jax.shard_map(
        body, mesh=mesh, in_specs=in_specs, out_specs=out_specs, check_vma=False
    )
```
